32 devices in a mesh: fsdp: 4 (over z), tp: 2 (over x), grp: 4 (over y, core).
Axes of the slice: x: 2, y: 2, z: 4, core: 2. Of those that a mesh axis runs over, the one named last changes fastest.
Arguments:
- hidden_states: bfloat16 [8, 1024, 4608], P(None, ('fsdp', 'grp'), 'tp'), may hold values from -6 to 6
- pre_gain: float32 [4608], replicated, may hold values from 0.25 to 1.75
- post_gain: float32 [4608], P('tp'), may hold values from 0.25 to 1.75
- query_weight: float32 [4608, 2048], P(('fsdp', 'grp'), 'tp'), may hold values from -0.09375 to 0.09375
- query_mean: float32 [4608, 2048], P(('fsdp', 'grp'), 'tp'), may hold values from -3 to 3
- query_square: float32 [4608, 2048], P(('fsdp', 'grp'), 'tp'), may hold values from 0.04 to 1
- query_gradient: bfloat16 [4608, 2048], P(('fsdp', 'grp'), 'tp'), may hold values from -6 to 6
- key_value_master_weight: float32 [4608, 2, 1024], P(('fsdp', 'grp'), None, 'tp'), may hold values from -0.09375 to 0.09375
- key_value_first_moment: float32 [4608, 2, 1024], P(('fsdp', 'grp'), None, 'tp'), may hold values from -3 to 3
- key_value_second_moment: float32 [4608, 2, 1024], P(('fsdp', 'grp'), None, 'tp'), may hold values from 0.04 to 1
- key_value_gradient: bfloat16 [4608, 2, 1024], P(('fsdp', 'grp'), None, 'tp'), may hold values from -6 to 6
- output_weight: float32 [4608, 2048], P(('fsdp', 'grp'), 'tp'), may hold values from -0.125 to 0.125
- output_mean: float32 [4608, 2048], P(('fsdp', 'grp'), 'tp'), may hold values from -3 to 3
- output_square: float32 [4608, 2048], P(('fsdp', 'grp'), 'tp'), may hold values from 0.04 to 1
- output_gradient: bfloat16 [4608, 2048], P(('fsdp', 'grp'), 'tp'), may hold values from -6 to 6
- stored_key_value_rows: bfloat16 [2, 1024, 64, 1024], P(None, ('fsdp', 'grp'), None, 'tp'), may hold values from -120 to 120
- lengths: int32 [1024], P(('fsdp', 'grp')), may hold values from 1 to 64
Outputs:
- rollout_states: bfloat16 [8, 1024, 4608], P(None, ('fsdp', 'grp'), 'tp')
- query_weight_next: float32 [4608, 2048], P(('fsdp', 'grp'), 'tp')
- query_mean_next: float32 [4608, 2048], P(('fsdp', 'grp'), 'tp')
- query_square_next: float32 [4608, 2048], P(('fsdp', 'grp'), 'tp')
- pair_weight_next: float32 [4608, 2, 1024], P(('fsdp', 'grp'), None, 'tp')
- pair_mean_next: float32 [4608, 2, 1024], P(('fsdp', 'grp'), None, 'tp')
- pair_square_next: float32 [4608, 2, 1024], P(('fsdp', 'grp'), None, 'tp')
- output_weight_next: float32 [4608, 2048], P(('fsdp', 'grp'), 'tp')
- output_mean_next: float32 [4608, 2048], P(('fsdp', 'grp'), 'tp')
- output_square_next: float32 [4608, 2048], P(('fsdp', 'grp'), 'tp')
The draws below stay inside these ranges and needn't reach their ends.
Inputs may be any that keep to these rules, and one draw needn't show every extreme that they name: lengths[r] cached positions of row r hold data; positions from lengths[r] on are ignored.
All inputs are finite; a program needn't handle non-finite values.
Results may differ from the reference program's by a relative error of at most 0.0074.
Values may be sent and summed in bfloat16 or wider, within the bound.
No kernel may reach another device: no remote copies, remote signals or barrier semaphores. Data moves between devices by JAX's collectives and lax.ppermute only.
A program may use at most 192 MiB of HBM per device.

```python
import math
import jax
import jax.numpy as jnp
from jax import lax

MODEL_WIDTH = 4608
HQ = 16
KEY_VALUE_HEADS = 8
HEAD_SIZE = 128
DECODE_STEPS = 8
CACHE_POSITIONS = 64
DECODED_ROWS = 1024


def draw_stored_key_value_rows(key, part):
    key = jax.random.fold_in(key, 5)
    key_start_offset = jax.random.fold_in(key, 1)
    key_pick = jax.random.fold_in(key, 2)
    base_offset = jax.random.normal(key_start_offset, (2, DECODED_ROWS, CACHE_POSITIONS, KEY_VALUE_HEADS * HEAD_SIZE), jnp.float32)
    base_offset = jnp.clip(base_offset, -6.0, 6.0)
    order = jax.random.permutation(key_pick, DECODED_ROWS)
    picked = order < DECODED_ROWS // 8
    key_scale = jnp.where(picked, 20.0, 1.0).astype(jnp.float32)
    side_scale = jnp.stack([key_scale, jnp.ones((DECODED_ROWS,), jnp.float32)], axis=0)
    return (base_offset * side_scale[:, :, None, None]).astype(jnp.bfloat16)


def set_ends(values, key, smallest, top_value):
    dims = values.shape
    spot = [jax.random.randint(jax.random.fold_in(key, axis), (), 0, dims[axis]) for axis in range(len(dims))]
    values = values.at[tuple(spot)].set(smallest)
    longest = dims.index(max(dims))
    spot[longest] = (spot[longest] + 1) % dims[longest]
    return values.at[tuple(spot)].set(top_value)


def steps_of(rng, dims, shards, least, largest):
    def one(axis_at, shards_of):
        steps = jax.random.uniform(jax.random.fold_in(jax.random.fold_in(rng, 6), axis_at), (shards_of,), jnp.float32, least / len(shards), largest / len(shards))
        return jnp.repeat(jnp.exp(steps), dims[axis_at] // shards_of).reshape((-1,) + (1,) * (len(dims) - axis_at - 1))

    loudness = one(*shards[0])
    for cut in shards[1:]:
        loudness = loudness * one(*cut)
    return loudness


def gaussian(stream_key, dims, width, bound, pieces=(), kind=jnp.bfloat16):
    gain = steps_of(stream_key, dims, pieces, -0.22, 0.18) if pieces else 1.0
    array = jax.random.normal(stream_key, dims, jnp.float32) * width * gain
    return jnp.minimum(jnp.maximum(array, -bound), bound).astype(kind)


def setup_inputs(seed: int = 0) -> dict:
    splits = jax.random.split(jax.random.key(seed), 18)
    hidden_states = gaussian(splits[0], (DECODE_STEPS, DECODED_ROWS, MODEL_WIDTH), 1.0, 6.0, ((1, 16), (2, 2)))
    pre_gain = jnp.clip(1.0 + 0.15 * jax.random.normal(splits[1], (MODEL_WIDTH,), jnp.float32), 0.25, 1.75)
    post_gain = jnp.clip(1.0 + 0.15 * jax.random.normal(splits[2], (MODEL_WIDTH,), jnp.float32), 0.25, 1.75)
    query_weight = gaussian(splits[3], (MODEL_WIDTH, HQ * HEAD_SIZE), MODEL_WIDTH ** -0.5, 0.09375, ((0, 16), (1, 2)), jnp.float32)
    query_mean = gaussian(splits[4], (MODEL_WIDTH, HQ * HEAD_SIZE), 0.5, 3.0, ((0, 16), (1, 2)), jnp.float32)
    query_square = jnp.clip(jnp.exp(math.log(1.0) - 3.218876 * jax.random.uniform(splits[5], (MODEL_WIDTH, HQ * HEAD_SIZE), jnp.float32) ** steps_of(splits[5], (MODEL_WIDTH, HQ * HEAD_SIZE), ((0, 16), (1, 2)), -0.2, 0.2)), 0.04, 1.0)
    query_gradient = gaussian(splits[6], (MODEL_WIDTH, HQ * HEAD_SIZE), 1.0, 6.0, ((0, 16), (1, 2)))
    key_value_master_weight = gaussian(splits[7], (MODEL_WIDTH, 2, KEY_VALUE_HEADS * HEAD_SIZE), MODEL_WIDTH ** -0.5, 0.09375, ((0, 16), (2, 2)), jnp.float32)
    key_value_first_moment = gaussian(splits[8], (MODEL_WIDTH, 2, KEY_VALUE_HEADS * HEAD_SIZE), 0.5, 3.0, ((0, 16), (2, 2)), jnp.float32)
    key_value_second_moment = jnp.clip(jnp.exp(math.log(1.0) - 3.218876 * jax.random.uniform(splits[9], (MODEL_WIDTH, 2, KEY_VALUE_HEADS * HEAD_SIZE), jnp.float32) ** steps_of(splits[9], (MODEL_WIDTH, 2, KEY_VALUE_HEADS * HEAD_SIZE), ((0, 16), (2, 2)), -0.2, 0.2)), 0.04, 1.0)
    key_value_gradient = gaussian(splits[10], (MODEL_WIDTH, 2, KEY_VALUE_HEADS * HEAD_SIZE), 1.0, 6.0, ((0, 16), (2, 2)))
    output_weight = gaussian(splits[11], (MODEL_WIDTH, HQ * HEAD_SIZE), (HQ * HEAD_SIZE) ** -0.5, 0.125, ((0, 16), (1, 2)), jnp.float32)
    output_mean = gaussian(splits[12], (MODEL_WIDTH, HQ * HEAD_SIZE), 0.5, 3.0, ((0, 16), (1, 2)), jnp.float32)
    output_square = jnp.clip(jnp.exp(math.log(1.0) - 3.218876 * jax.random.uniform(splits[13], (MODEL_WIDTH, HQ * HEAD_SIZE), jnp.float32) ** steps_of(splits[13], (MODEL_WIDTH, HQ * HEAD_SIZE), ((0, 16), (1, 2)), -0.2, 0.2)), 0.04, 1.0)
    output_gradient = gaussian(splits[14], (MODEL_WIDTH, HQ * HEAD_SIZE), 1.0, 6.0, ((0, 16), (1, 2)))
    stored_key_value_rows = draw_stored_key_value_rows(jax.random.fold_in(splits[17], 71), 0)
    lengths = set_ends(jax.random.randint(splits[16], (DECODED_ROWS,), 1, CACHE_POSITIONS + 1), jax.random.fold_in(splits[16], 1), 1, CACHE_POSITIONS).astype(jnp.int32)
    return dict(hidden_states=hidden_states, pre_gain=pre_gain, post_gain=post_gain, query_weight=query_weight, query_mean=query_mean, query_square=query_square, query_gradient=query_gradient, key_value_master_weight=key_value_master_weight, key_value_first_moment=key_value_first_moment, key_value_second_moment=key_value_second_moment, key_value_gradient=key_value_gradient, output_weight=output_weight, output_mean=output_mean, output_square=output_square, output_gradient=output_gradient, stored_key_value_rows=stored_key_value_rows, lengths=lengths)


beta_first = 0.9
beta_second = 0.95
learning_rate = 0.001
update_number = 100
soft_limit = 50.0
query_factor = 144.0 ** (-0.5)
norm_epsilon = 1e-06

def adam_update(master, moment_mean, moment_square, gradient):
    gradient_float = gradient.astype(jnp.float32)
    mean_next = beta_first * moment_mean + (1.0 - beta_first) * gradient_float
    square_next = beta_second * moment_square + (1.0 - beta_second) * gradient_float * gradient_float
    mean_hat = mean_next / (1.0 - beta_first ** update_number)
    square_hat = square_next / (1.0 - beta_second ** update_number)
    master_next = master - learning_rate * mean_hat / jnp.sqrt(square_hat)
    return (master_next, mean_next, square_next)

def rms_apply(values, gains):
    mean_square = lax.optimization_barrier(jnp.mean(values * values, axis=-1, keepdims=True)) + norm_epsilon
    return values * lax.rsqrt(mean_square) * gains

def attend(query_rows, new_keys, new_values, cache_keys, cache_values, lengths):
    step_count = query_rows.shape[0]
    cache_count = cache_keys.shape[1]
    query_float = query_rows.astype(jnp.float32)
    score_cache = jnp.einsum('trgqd,rcgd->trgqc', query_float, cache_keys.astype(jnp.float32))
    score_fresh = jnp.einsum('trgqd,srgd->trgqs', query_float, new_keys.astype(jnp.float32))
    score_cache = soft_limit * jnp.tanh(score_cache * query_factor / soft_limit)
    score_fresh = soft_limit * jnp.tanh(score_fresh * query_factor / soft_limit)
    live_cache = jnp.arange(cache_count, dtype=jnp.int32)[None, :] < lengths[:, None]
    positions = jnp.arange(step_count, dtype=jnp.int32)
    live_fresh = positions[None, :] <= positions[:, None]
    weight_cache = jnp.where(live_cache[None, :, None, None, :], jnp.exp(score_cache), 0.0)
    weight_fresh = jnp.where(live_fresh[:, None, None, None, :], jnp.exp(score_fresh), 0.0)
    totals = lax.optimization_barrier(jnp.sum(weight_cache, axis=-1, keepdims=True)) + lax.optimization_barrier(jnp.sum(weight_fresh, axis=-1, keepdims=True))
    prob_cache = (weight_cache / totals).astype(jnp.bfloat16)
    prob_fresh = (weight_fresh / totals).astype(jnp.bfloat16)
    mixed = jnp.einsum('trgqc,rcgd->trgqd', prob_cache.astype(jnp.float32), cache_values.astype(jnp.float32))
    mixed = mixed + jnp.einsum('trgqs,srgd->trgqd', prob_fresh.astype(jnp.float32), new_values.astype(jnp.float32))
    return mixed.astype(jnp.bfloat16)

def reference(hidden_states, pre_gain, post_gain, query_weight, query_mean, query_square, query_gradient, key_value_master_weight, key_value_first_moment, key_value_second_moment, key_value_gradient, output_weight, output_mean, output_square, output_gradient, stored_key_value_rows, lengths):
    query_next = adam_update(query_weight, query_mean, query_square, query_gradient)
    key_value_following = adam_update(key_value_master_weight, key_value_first_moment, key_value_second_moment, key_value_gradient)
    output_next = adam_update(output_weight, output_mean, output_square, output_gradient)
    query_matrix = query_next[0].astype(jnp.bfloat16)
    key_value_matrix = key_value_following[0].astype(jnp.bfloat16).reshape(MODEL_WIDTH, 2 * KEY_VALUE_HEADS * HEAD_SIZE)
    output_matrix = output_next[0].astype(jnp.bfloat16)
    states = hidden_states.astype(jnp.float32)
    normed = rms_apply(states, pre_gain).astype(jnp.bfloat16).reshape(DECODE_STEPS * DECODED_ROWS, MODEL_WIDTH)
    query_rows = jnp.dot(normed, query_matrix, preferred_element_type=jnp.float32).astype(jnp.bfloat16)
    key_value_items = jnp.dot(normed, key_value_matrix, preferred_element_type=jnp.float32).astype(jnp.bfloat16)
    query_rows = query_rows.reshape(DECODE_STEPS, DECODED_ROWS, KEY_VALUE_HEADS, 2, HEAD_SIZE)
    key_value_items = key_value_items.reshape(DECODE_STEPS, DECODED_ROWS, 2, KEY_VALUE_HEADS, HEAD_SIZE)
    cache_division = stored_key_value_rows.reshape(2, DECODED_ROWS, CACHE_POSITIONS, KEY_VALUE_HEADS, HEAD_SIZE)
    mixed = attend(query_rows, key_value_items[:, :, 0], key_value_items[:, :, 1], cache_division[0], cache_division[1], lengths)
    mixed = mixed.reshape(DECODE_STEPS * DECODED_ROWS, HQ * HEAD_SIZE)
    projected = jnp.dot(mixed, output_matrix.T, preferred_element_type=jnp.float32)
    branch = rms_apply(projected, post_gain).reshape(DECODE_STEPS, DECODED_ROWS, MODEL_WIDTH)
    rollout_states = (states + branch).astype(jnp.bfloat16)
    return (rollout_states, query_next[0], query_next[1], query_next[2], key_value_following[0], key_value_following[1], key_value_following[2], output_next[0], output_next[1], output_next[2])
```

```python
import functools

import jax
import jax.numpy as jnp
from jax import lax
from jax.experimental import pallas as pl
from jax.experimental.pallas import tpu as pltpu
from jax.sharding import PartitionSpec as P

HEAD_SIZE = 128


beta_first = 0.9
beta_second = 0.95
learning_rate = 0.001
update_number = 100
soft_limit = 50.0
query_factor = 144.0 ** (-0.5)
norm_epsilon = 1e-06


def adam_update(master, moment_mean, moment_square, gradient):
    gradient_float = gradient.astype(jnp.float32)
    mean_next = beta_first * moment_mean + (1.0 - beta_first) * gradient_float
    square_next = (
        beta_second * moment_square + (1.0 - beta_second) * gradient_float * gradient_float
    )
    mean_hat = mean_next / (1.0 - beta_first**update_number)
    square_hat = square_next / (1.0 - beta_second**update_number)
    master_next = master - learning_rate * mean_hat / jnp.sqrt(square_hat)
    return (master_next, mean_next, square_next)


def rms_apply(values, gains):
    mean_square = jnp.mean(values * values, axis=-1, keepdims=True) + norm_epsilon
    return values * lax.rsqrt(mean_square) * gains


def attend(query_rows, new_keys, new_values, cache_keys, cache_values, lengths):
    step_count = query_rows.shape[0]
    cache_count = cache_keys.shape[1]
    score_cache = jnp.einsum(
        "trgqd,rcgd->trgqc", query_rows, cache_keys, preferred_element_type=jnp.float32
    )
    score_fresh = jnp.einsum(
        "trgqd,srgd->trgqs", query_rows, new_keys, preferred_element_type=jnp.float32
    )
    score_cache = soft_limit * jnp.tanh(score_cache * query_factor / soft_limit)
    score_fresh = soft_limit * jnp.tanh(score_fresh * query_factor / soft_limit)
    live_cache = jnp.arange(cache_count, dtype=jnp.int32)[None, :] < lengths[:, None]
    positions = jnp.arange(step_count, dtype=jnp.int32)
    live_fresh = positions[None, :] <= positions[:, None]
    weight_cache = jnp.where(live_cache[None, :, None, None, :], jnp.exp(score_cache), 0.0)
    weight_fresh = jnp.where(live_fresh[:, None, None, None, :], jnp.exp(score_fresh), 0.0)
    totals = jnp.sum(weight_cache, axis=-1, keepdims=True) + jnp.sum(
        weight_fresh, axis=-1, keepdims=True
    )
    prob_cache = (weight_cache / totals).astype(jnp.bfloat16)
    prob_fresh = (weight_fresh / totals).astype(jnp.bfloat16)
    mixed = jnp.einsum(
        "trgqc,rcgd->trgqd", prob_cache, cache_values, preferred_element_type=jnp.float32
    )
    mixed = mixed + jnp.einsum(
        "trgqs,srgd->trgqd", prob_fresh, new_values, preferred_element_type=jnp.float32
    )
    return mixed.astype(jnp.bfloat16)


def per_device(
    hidden_states,
    pre_gain,
    post_gain,
    query_weight,
    query_mean,
    query_square,
    query_gradient,
    key_value_master_weight,
    key_value_first_moment,
    key_value_second_moment,
    key_value_gradient,
    output_weight,
    output_mean,
    output_square,
    output_gradient,
    stored_key_value_rows,
    lengths,
):
    query_next = adam_update(query_weight, query_mean, query_square, query_gradient)
    key_value_following = adam_update(
        key_value_master_weight, key_value_first_moment, key_value_second_moment, key_value_gradient
    )
    output_next = adam_update(output_weight, output_mean, output_square, output_gradient)
    query_matrix = query_next[0].astype(jnp.bfloat16)
    key_value_matrix = key_value_following[0].astype(jnp.bfloat16)
    key_value_matrix = key_value_matrix.reshape(key_value_matrix.shape[0], -1)
    output_matrix = output_next[0].astype(jnp.bfloat16)
    gathered = lax.all_gather(hidden_states, "tp", axis=2, tiled=True)
    step_count, row_count, full_width = gathered.shape
    token_count = step_count * row_count
    normed = (
        rms_apply(gathered.astype(jnp.float32), pre_gain)
        .astype(jnp.bfloat16)
        .reshape(token_count, full_width)
    )
    query_sum = jnp.dot(
        normed,
        lax.all_gather(query_matrix, ("fsdp", "grp"), axis=0, tiled=True),
        preferred_element_type=jnp.float32,
    )
    pair_sum = jnp.dot(
        normed,
        lax.all_gather(key_value_matrix, ("fsdp", "grp"), axis=0, tiled=True),
        preferred_element_type=jnp.float32,
    )
    group_count = stored_key_value_rows.shape[-1] // HEAD_SIZE
    cache_count = stored_key_value_rows.shape[2]
    query_rows = query_sum.astype(jnp.bfloat16).reshape(
        step_count, row_count, group_count, 2, HEAD_SIZE
    )
    key_value_items = pair_sum.astype(jnp.bfloat16).reshape(
        step_count, row_count, 2, group_count, HEAD_SIZE
    )
    cache_division = stored_key_value_rows.reshape(
        2, row_count, cache_count, group_count, HEAD_SIZE
    )
    mixed = attend(
        query_rows,
        key_value_items[:, :, 0],
        key_value_items[:, :, 1],
        cache_division[0],
        cache_division[1],
        lengths,
    )
    mixed = mixed.reshape(token_count, group_count * 2 * HEAD_SIZE)
    projected = lax.dot_general(
        mixed,
        lax.all_gather(output_matrix, ("fsdp", "grp"), axis=0, tiled=True),
        (((1,), (1,)), ((), ())),
        preferred_element_type=jnp.float32,
    )
    shares = lax.psum_scatter(projected, "tp", scatter_dimension=1, tiled=True)
    row_squares = jnp.sum(shares * shares, axis=1)
    square_total = lax.psum(row_squares, "tp")
    inverse = lax.rsqrt(square_total / full_width + norm_epsilon)
    branch = shares * inverse[:, None] * post_gain
    rollout_states = (
        hidden_states.astype(jnp.float32) + branch.reshape(step_count, row_count, -1)
    ).astype(jnp.bfloat16)
    return (
        rollout_states,
        query_next[0],
        query_next[1],
        query_next[2],
        key_value_following[0],
        key_value_following[1],
        key_value_following[2],
        output_next[0],
        output_next[1],
        output_next[2],
    )


def ring(values, count):
    return lax.ppermute(values, "fsdp", [(i, (i + 1) % count) for i in range(count)])


def flip(values, bit):
    return lax.ppermute(values, "grp", [(i, i ^ bit) for i in range(4)])


def across(values):
    return lax.ppermute(values, "tp", [(0, 1), (1, 0)])


def plane_gather(block, count):
    held = [block]
    for _ in range(count - 1):
        held.append(ring(held[-1], count))
    swapped = [flip(values, 2) for values in held]
    return [(k, 0, values) for k, values in enumerate(held)] + [
        (k, 1, values) for k, values in enumerate(swapped)
    ]


def qkv_kernel(places, count, depth, own_ref, other_ref, *refs):
    slots = refs[: len(places)]
    out_ref, weights, sems = refs[len(places) :]
    step = pl.program_id(0)
    tile = out_ref.shape[1]
    half = count // 2
    front = lax.axis_index("fsdp")
    side = lax.axis_index("tp")
    inner = lax.axis_index("grp")
    row, core = inner // 2, inner % 2

    def copies(index):
        columns = pl.ds(index * tile, tile)
        for number, ((k, dy), slot) in enumerate(zip(places, slots)):
            source = lax.rem(front - k + count, count)
            part = lax.rem(source // half + side, 2)
            base = (part * half + lax.rem(source, half)) * 4 + lax.rem(row + dy, 2) * 2
            for dc in range(2):
                start = pl.multiple_of((base + lax.rem(core + dc, 2)) * depth, depth)
                yield pltpu.make_async_copy(
                    slot.at[pl.ds(dc * depth, depth), columns],
                    weights.at[index, pl.ds(start, depth), :],
                    sems.at[index, number * 2 + dc],
                )

    tiles = weights.shape[0]

    @pl.when(step == 0)
    def _():
        for index in range(tiles):
            for copy in copies(index):
                copy.start()

    for index in range(tiles):

        @pl.when(step == index)
        def _(index=index):
            for copy in copies(index):
                copy.wait()

    width = own_ref.shape[1]

    def rows(m, carry):
        at = pl.ds(pl.multiple_of(m * 128, 128), 128)
        total = jnp.dot(
            own_ref[at, :], weights[step, :width, :], preferred_element_type=jnp.float32
        )
        total += jnp.dot(
            other_ref[at, :], weights[step, width:, :], preferred_element_type=jnp.float32
        )
        out_ref[at, :] = total.astype(out_ref.dtype)
        return carry

    lax.fori_loop(0, out_ref.shape[0] // 128, rows, 0)


def qkv_matmul(own, other, slots, count):
    tokens, width = own.shape
    depth, columns = slots[0][2].shape[0] // 2, slots[0][2].shape[1]
    tile = 256
    places = [(k, dy) for k, dy, _ in slots]
    whole = pl.BlockSpec((tokens, width), lambda n: (0, 0))
    return pl.pallas_call(
        functools.partial(qkv_kernel, places, count, depth),
        out_shape=jax.ShapeDtypeStruct((tokens, columns), jnp.bfloat16),
        grid=(columns // tile,),
        in_specs=[whole, whole] + [pl.BlockSpec(memory_space=pl.ANY)] * len(slots),
        out_specs=pl.BlockSpec((tokens, tile), lambda n: (0, n)),
        scratch_shapes=[
            pltpu.VMEM((columns // tile, 2 * width, tile), jnp.bfloat16),
            pltpu.SemaphoreType.DMA((columns // tile, 2 * len(slots))),
        ],
        compiler_params=pltpu.CompilerParams(vmem_limit_bytes=40 * 2**20),
        cost_estimate=pl.CostEstimate(
            flops=4 * tokens * width * columns,
            bytes_accessed=4 * width * (tokens + columns) + 2 * tokens * columns,
            transcendentals=0,
        ),
    )(own, other, *[values for _, _, values in slots])


def out_kernel(places, count, depth, own_ref, other_ref, *refs):
    slots = refs[: len(places)]
    out_ref, square_ref, weights, sems = refs[len(places) :]
    step = pl.program_id(0)
    half = count // 2
    front = lax.axis_index("fsdp")
    side = lax.axis_index("tp")
    inner = lax.axis_index("grp")
    row, core = inner // 2, inner % 2
    width = own_ref.shape[1]

    def copies():
        for number, ((k, dy, dc), slot) in enumerate(zip(places, slots)):
            source = lax.rem(front - k + count, count)
            part = lax.rem(source // half + side, 2)
            base = lax.rem(source, half) * 4 + lax.rem(row + dy, 2) * 2
            start = pl.multiple_of((base + lax.rem(core + dc, 2)) * depth, depth)
            yield pltpu.make_async_copy(
                slot, weights.at[part, pl.ds(start, depth), :], sems.at[number]
            )

    @pl.when(step == 0)
    def _():
        for copy in copies():
            copy.start()
        for copy in copies():
            copy.wait()

    tile = out_ref.shape[1]
    piece = tile // 3
    contract = (((1,), (1,)), ((), ()))

    def rows(m, carry):
        at = pl.ds(pl.multiple_of(m * 128, 128), 128)
        squares = jnp.zeros((128, 1), jnp.float32)
        for n in range(3):
            start = pl.multiple_of(step * tile + n * piece, piece)
            total = lax.dot_general(
                own_ref[at, :],
                weights[0, pl.ds(start, piece), :],
                contract,
                preferred_element_type=jnp.float32,
            )
            total += lax.dot_general(
                other_ref[at, :],
                weights[1, pl.ds(start, piece), :],
                contract,
                preferred_element_type=jnp.float32,
            )
            out_ref[at, pl.ds(n * piece, piece)] = total
            squares += jnp.sum(total * total, axis=1, keepdims=True)

        @pl.when(step == 0)
        def _():
            square_ref[at, :] = squares

        @pl.when(step > 0)
        def _():
            square_ref[at, :] += squares

        return carry

    lax.fori_loop(0, out_ref.shape[0] // 128, rows, 0)


def out_matmul(own, other, slots, count):
    tokens, width = own.shape
    depth = slots[0][1].shape[0]
    groups = count // 2
    features = groups * 4 * depth
    whole = pl.BlockSpec((tokens, width), lambda n: (0, 0))
    return pl.pallas_call(
        functools.partial(out_kernel, [place for place, _ in slots], count, depth),
        out_shape=(
            jax.ShapeDtypeStruct((tokens, features), jnp.float32),
            jax.ShapeDtypeStruct((tokens, 1), jnp.float32),
        ),
        grid=(groups,),
        in_specs=[whole, whole] + [pl.BlockSpec(memory_space=pl.ANY)] * len(slots),
        out_specs=(
            pl.BlockSpec((tokens, 4 * depth), lambda n: (0, n)),
            pl.BlockSpec((tokens, 1), lambda n: (0, 0)),
        ),
        scratch_shapes=[
            pltpu.VMEM((2, features, width), jnp.bfloat16),
            pltpu.SemaphoreType.DMA((len(slots),)),
        ],
        compiler_params=pltpu.CompilerParams(vmem_limit_bytes=40 * 2**20),
        cost_estimate=pl.CostEstimate(
            flops=4 * tokens * width * features,
            bytes_accessed=4 * width * (tokens + features) + 4 * tokens * features,
            transcendentals=0,
        ),
    )(own, other, *[values for _, values in slots])


def per_device_plane(
    count,
    hidden_states,
    pre_gain,
    post_gain,
    query_weight,
    query_mean,
    query_square,
    query_gradient,
    key_value_master_weight,
    key_value_first_moment,
    key_value_second_moment,
    key_value_gradient,
    output_weight,
    output_mean,
    output_square,
    output_gradient,
    stored_key_value_rows,
    lengths,
):
    side = lax.axis_index("tp")
    core = lax.axis_index("grp") % 2
    half = count // 2
    step_count, row_count, width = hidden_states.shape
    token_count = step_count * row_count
    group_count = stored_key_value_rows.shape[-1] // HEAD_SIZE
    cache_count = stored_key_value_rows.shape[2]
    states = hidden_states.reshape(token_count, width)

    far_states = across(states)
    query_next = adam_update(query_weight, query_mean, query_square, query_gradient)
    key_value_following = adam_update(
        key_value_master_weight, key_value_first_moment, key_value_second_moment, key_value_gradient
    )
    output_next = adam_update(output_weight, output_mean, output_square, output_gradient)

    query_matrix = query_next[0].astype(jnp.bfloat16)
    pair_matrix = key_value_following[0].astype(jnp.bfloat16)
    halves = []
    for side_of in range(2):
        wide = query_matrix.shape[1] // 2
        narrow = pair_matrix.shape[2] // 2
        halves.append(
            jnp.concatenate(
                [
                    query_matrix[:, side_of * wide : (side_of + 1) * wide],
                    pair_matrix[:, 0, side_of * narrow : (side_of + 1) * narrow],
                    pair_matrix[:, 1, side_of * narrow : (side_of + 1) * narrow],
                ],
                axis=1,
            )
        )
    kept = jnp.where(core == 0, halves[0], halves[1])
    given = jnp.where(core == 0, halves[1], halves[0])
    block = jnp.concatenate([kept, flip(given, 1)], axis=0)
    slots = plane_gather(block, count)

    output_matrix = output_next[0].astype(jnp.bfloat16)
    moves = []
    for front in range(count):
        for at in range(2):
            if front // half == at:
                moves.append((front * 2 + at, front * 2 + at))
            else:
                moves.append((front * 2 + at, (front + half) % count * 2 + 1 - at))
    moved = lax.ppermute(output_matrix, ("fsdp", "tp"), moves)
    output_slots = []
    for k, dy, values in plane_gather(moved, count):
        output_slots.append(((k, dy, 0), values))
        output_slots.append(((k, dy, 1), flip(values, 1)))

    near = states.astype(jnp.float32)
    far = far_states.astype(jnp.float32)
    mean_square = (
        jnp.sum(near * near, axis=1, keepdims=True) + jnp.sum(far * far, axis=1, keepdims=True)
    ) / (2 * width)
    scale = lax.rsqrt(mean_square + norm_epsilon)
    near_gain = lax.dynamic_slice_in_dim(pre_gain, side * width, width)
    far_gain = lax.dynamic_slice_in_dim(pre_gain, (1 - side) * width, width)
    near_normed = (near * scale * near_gain).astype(jnp.bfloat16)
    far_normed = (far * scale * far_gain).astype(jnp.bfloat16)
    away = qkv_matmul(flip(near_normed, 1), flip(far_normed, 1), slots, count)
    back = flip(away, 1)
    home = qkv_matmul(near_normed, far_normed, slots, count)
    low = jnp.where(core == 0, home, back)
    high = jnp.where(core == 0, back, home)
    quarter = home.shape[1] // 4

    def heads(start, stop):
        joined = jnp.concatenate([low[:, start:stop], high[:, start:stop]], axis=1)
        return joined.reshape(step_count, row_count, group_count, -1, HEAD_SIZE)

    query_rows = heads(0, 2 * quarter)
    new_keys = heads(2 * quarter, 3 * quarter)[:, :, :, 0]
    new_values = heads(3 * quarter, 4 * quarter)[:, :, :, 0]
    cache_division = stored_key_value_rows.reshape(
        2, row_count, cache_count, group_count, HEAD_SIZE
    )
    mixed = attend(
        query_rows, new_keys, new_values, cache_division[0], cache_division[1], lengths
    ).reshape(token_count, group_count * 2 * HEAD_SIZE)
    projected, squares = out_matmul(mixed, across(mixed), output_slots, count)
    square_total = squares + across(squares)
    inverse = lax.rsqrt(square_total / (2 * width) + norm_epsilon)
    branch = projected * inverse * post_gain
    rollout_states = (states.astype(jnp.float32) + branch).astype(jnp.bfloat16)
    return (
        rollout_states.reshape(hidden_states.shape),
        *query_next,
        *key_value_following,
        *output_next,
    )


def plan_for(mesh, depth):
    sizes = dict(mesh.shape)
    count = sizes["fsdp"]
    rows = depth // (count * sizes["grp"])
    if sizes["tp"] == 2 and sizes["grp"] == 4 and count % 2 == 0 and rows % 16 == 0:
        return functools.partial(per_device_plane, count)
    return per_device


def solution(mesh):
    placed = (
        P(None, ("fsdp", "grp"), "tp"),
        P(),
        P("tp"),
        P(("fsdp", "grp"), "tp"),
        P(("fsdp", "grp"), "tp"),
        P(("fsdp", "grp"), "tp"),
        P(("fsdp", "grp"), "tp"),
        P(("fsdp", "grp"), None, "tp"),
        P(("fsdp", "grp"), None, "tp"),
        P(("fsdp", "grp"), None, "tp"),
        P(("fsdp", "grp"), None, "tp"),
        P(("fsdp", "grp"), "tp"),
        P(("fsdp", "grp"), "tp"),
        P(("fsdp", "grp"), "tp"),
        P(("fsdp", "grp"), "tp"),
        P(None, ("fsdp", "grp"), None, "tp"),
        P(("fsdp", "grp")),
    )
    mapped = functools.partial(
        jax.shard_map,
        mesh=mesh,
        in_specs=placed,
        out_specs=(
            P(None, ("fsdp", "grp"), "tp"),
            P(("fsdp", "grp"), "tp"),
            P(("fsdp", "grp"), "tp"),
            P(("fsdp", "grp"), "tp"),
            P(("fsdp", "grp"), None, "tp"),
            P(("fsdp", "grp"), None, "tp"),
            P(("fsdp", "grp"), None, "tp"),
            P(("fsdp", "grp"), "tp"),
            P(("fsdp", "grp"), "tp"),
            P(("fsdp", "grp"), "tp"),
        ),
        check_vma=False,
    )

    def step(*args):
        return mapped(plan_for(mesh, args[3].shape[0]))(*args)

    return step
```

```python
import functools

import jax
import jax.numpy as jnp
from jax import lax
from jax.experimental import pallas as pl
from jax.experimental.pallas import tpu as pltpu
from jax.sharding import PartitionSpec as P

HEAD_SIZE = 128


beta_first = 0.9
beta_second = 0.95
learning_rate = 0.001
update_number = 100
soft_limit = 50.0
query_factor = 144.0 ** (-0.5)
norm_epsilon = 1e-06


def adam_update(master, moment_mean, moment_square, gradient):
    gradient_float = gradient.astype(jnp.float32)
    mean_next = beta_first * moment_mean + (1.0 - beta_first) * gradient_float
    square_next = (
        beta_second * moment_square + (1.0 - beta_second) * gradient_float * gradient_float
    )
    mean_hat = mean_next / (1.0 - beta_first**update_number)
    square_hat = square_next / (1.0 - beta_second**update_number)
    master_next = master - learning_rate * mean_hat / jnp.sqrt(square_hat)
    return (master_next, mean_next, square_next)


def rms_apply(values, gains):
    mean_square = jnp.mean(values * values, axis=-1, keepdims=True) + norm_epsilon
    return values * lax.rsqrt(mean_square) * gains


def attend(query_rows, new_keys, new_values, cache_keys, cache_values, lengths):
    step_count = query_rows.shape[0]
    cache_count = cache_keys.shape[1]
    score_cache = jnp.einsum(
        "trgqd,rcgd->trgqc", query_rows, cache_keys, preferred_element_type=jnp.float32
    )
    score_fresh = jnp.einsum(
        "trgqd,srgd->trgqs", query_rows, new_keys, preferred_element_type=jnp.float32
    )
    score_cache = soft_limit * jnp.tanh(score_cache * query_factor / soft_limit)
    score_fresh = soft_limit * jnp.tanh(score_fresh * query_factor / soft_limit)
    live_cache = jnp.arange(cache_count, dtype=jnp.int32)[None, :] < lengths[:, None]
    positions = jnp.arange(step_count, dtype=jnp.int32)
    live_fresh = positions[None, :] <= positions[:, None]
    weight_cache = jnp.where(live_cache[None, :, None, None, :], jnp.exp(score_cache), 0.0)
    weight_fresh = jnp.where(live_fresh[:, None, None, None, :], jnp.exp(score_fresh), 0.0)
    totals = jnp.sum(weight_cache, axis=-1, keepdims=True) + jnp.sum(
        weight_fresh, axis=-1, keepdims=True
    )
    prob_cache = (weight_cache / totals).astype(jnp.bfloat16)
    prob_fresh = (weight_fresh / totals).astype(jnp.bfloat16)
    mixed = jnp.einsum(
        "trgqc,rcgd->trgqd", prob_cache, cache_values, preferred_element_type=jnp.float32
    )
    mixed = mixed + jnp.einsum(
        "trgqs,srgd->trgqd", prob_fresh, new_values, preferred_element_type=jnp.float32
    )
    return mixed.astype(jnp.bfloat16)


def per_device(
    hidden_states,
    pre_gain,
    post_gain,
    query_weight,
    query_mean,
    query_square,
    query_gradient,
    key_value_master_weight,
    key_value_first_moment,
    key_value_second_moment,
    key_value_gradient,
    output_weight,
    output_mean,
    output_square,
    output_gradient,
    stored_key_value_rows,
    lengths,
):
    query_next = adam_update(query_weight, query_mean, query_square, query_gradient)
    key_value_following = adam_update(
        key_value_master_weight, key_value_first_moment, key_value_second_moment, key_value_gradient
    )
    output_next = adam_update(output_weight, output_mean, output_square, output_gradient)
    query_matrix = query_next[0].astype(jnp.bfloat16)
    key_value_matrix = key_value_following[0].astype(jnp.bfloat16)
    key_value_matrix = key_value_matrix.reshape(key_value_matrix.shape[0], -1)
    output_matrix = output_next[0].astype(jnp.bfloat16)
    gathered = lax.all_gather(hidden_states, "tp", axis=2, tiled=True)
    step_count, row_count, full_width = gathered.shape
    token_count = step_count * row_count
    normed = (
        rms_apply(gathered.astype(jnp.float32), pre_gain)
        .astype(jnp.bfloat16)
        .reshape(token_count, full_width)
    )
    query_sum = jnp.dot(
        normed,
        lax.all_gather(query_matrix, ("fsdp", "grp"), axis=0, tiled=True),
        preferred_element_type=jnp.float32,
    )
    pair_sum = jnp.dot(
        normed,
        lax.all_gather(key_value_matrix, ("fsdp", "grp"), axis=0, tiled=True),
        preferred_element_type=jnp.float32,
    )
    group_count = stored_key_value_rows.shape[-1] // HEAD_SIZE
    cache_count = stored_key_value_rows.shape[2]
    query_rows = query_sum.astype(jnp.bfloat16).reshape(
        step_count, row_count, group_count, 2, HEAD_SIZE
    )
    key_value_items = pair_sum.astype(jnp.bfloat16).reshape(
        step_count, row_count, 2, group_count, HEAD_SIZE
    )
    cache_division = stored_key_value_rows.reshape(
        2, row_count, cache_count, group_count, HEAD_SIZE
    )
    mixed = attend(
        query_rows,
        key_value_items[:, :, 0],
        key_value_items[:, :, 1],
        cache_division[0],
        cache_division[1],
        lengths,
    )
    mixed = mixed.reshape(token_count, group_count * 2 * HEAD_SIZE)
    projected = lax.dot_general(
        mixed,
        lax.all_gather(output_matrix, ("fsdp", "grp"), axis=0, tiled=True),
        (((1,), (1,)), ((), ())),
        preferred_element_type=jnp.float32,
    )
    shares = lax.psum_scatter(projected, "tp", scatter_dimension=1, tiled=True)
    row_squares = jnp.sum(shares * shares, axis=1)
    square_total = lax.psum(row_squares, "tp")
    inverse = lax.rsqrt(square_total / full_width + norm_epsilon)
    branch = shares * inverse[:, None] * post_gain
    rollout_states = (
        hidden_states.astype(jnp.float32) + branch.reshape(step_count, row_count, -1)
    ).astype(jnp.bfloat16)
    return (
        rollout_states,
        query_next[0],
        query_next[1],
        query_next[2],
        key_value_following[0],
        key_value_following[1],
        key_value_following[2],
        output_next[0],
        output_next[1],
        output_next[2],
    )


def flip(values, bit):
    return lax.ppermute(values, "grp", [(i, i ^ bit) for i in range(4)])


def across(values):
    return lax.ppermute(values, "tp", [(0, 1), (1, 0)])


def after(values, *others):
    return lax.optimization_barrier((values, *others))[0]


class Lanes:
    def __init__(self, count):
        self.count = count
        self.along_z = []
        self.along_y = []

    def ring(self, values, *others):
        step = len(self.along_z)
        waits = self.along_y[step - 2 : step - 1] if step > 1 else []
        values = after(values, *self.along_z[-2:-1], *waits, *others)
        moves = [(i, (i + 1) % self.count) for i in range(self.count)]
        self.along_z.append(lax.ppermute(values, "fsdp", moves))
        return self.along_z[-1]

    def swap(self, values, *others):
        values = after(values, *self.along_y[-2:-1], *others)
        self.along_y.append(flip(values, 2))
        return self.along_y[-1]


def qkv_kernel(places, count, depth, *refs):
    inputs, slots = refs[:4], refs[4 : 4 + len(places)]
    away_ref, home_ref, tokens, weights, token_sems, sems = refs[4 + len(places) :]
    half = count // 2
    front = lax.axis_index("fsdp")
    side = lax.axis_index("tp")
    inner = lax.axis_index("grp")
    row, core = inner // 2, lax.rem(inner, 2)
    tiles, _, tile = weights.shape
    width = inputs[0].shape[1]

    def bring_tokens(group):
        for part in range(2):
            yield pltpu.make_async_copy(
                inputs[2 * group + part],
                tokens.at[group, :, pl.ds(part * width, width)],
                token_sems.at[group, part],
            )

    def bring_weights(index):
        for number, ((k, dy), slot) in enumerate(zip(places, slots)):
            source = lax.rem(front - k + count, count)
            part = lax.rem(source // half + side, 2)
            base = (part * half + lax.rem(source, half)) * 4 + lax.rem(row + dy, 2) * 2
            for dc in range(2):
                start = pl.multiple_of((base + lax.rem(core + dc, 2)) * depth, depth)
                yield pltpu.make_async_copy(
                    slot.at[pl.ds(dc * depth, depth), pl.ds(index * tile, tile)],
                    weights.at[index, pl.ds(start, depth), :],
                    sems.at[index, number * 2 + dc],
                )

    def start(copies):
        for copy in copies:
            copy.start()

    def wait(copies):
        for copy in copies:
            copy.wait()

    start(bring_weights(0))
    start(bring_tokens(0))
    for index in range(1, tiles):
        start(bring_weights(index))
    start(bring_tokens(1))
    for group, out_ref in enumerate((away_ref, home_ref)):
        wait(bring_tokens(group))
        for index in range(tiles):
            if group == 0:
                wait(bring_weights(index))
            out_ref[:, index * tile : (index + 1) * tile] = jnp.dot(
                tokens[group], weights[index], preferred_element_type=jnp.float32
            ).astype(out_ref.dtype)


def qkv_matmul(away, home, slots, count):
    tokens, width = home[0].shape
    depth, columns = slots[0][2].shape[0] // 2, slots[0][2].shape[1]
    tile = 256
    return pl.pallas_call(
        functools.partial(qkv_kernel, [(k, dy) for k, dy, _ in slots], count, depth),
        out_shape=(jax.ShapeDtypeStruct((tokens, columns), jnp.bfloat16),) * 2,
        in_specs=[pl.BlockSpec(memory_space=pltpu.HBM)] * (4 + len(slots)),
        out_specs=(pl.BlockSpec(memory_space=pltpu.VMEM),) * 2,
        scratch_shapes=[
            pltpu.VMEM((2, tokens, 2 * width), jnp.bfloat16),
            pltpu.VMEM((columns // tile, 2 * width, tile), jnp.bfloat16),
            pltpu.SemaphoreType.DMA((2, 2)),
            pltpu.SemaphoreType.DMA((columns // tile, 2 * len(slots))),
        ],
        compiler_params=pltpu.CompilerParams(vmem_limit_bytes=56 * 2**20),
        cost_estimate=pl.CostEstimate(
            flops=8 * tokens * width * columns,
            bytes_accessed=4 * width * (2 * tokens + columns) + 4 * tokens * columns,
            transcendentals=0,
        ),
    )(*away, *home, *[values for _, _, values in slots])


def attend_kernel(heads_ref, home_ref, back_ref, home_cache, back_cache, limit_ref, out_ref):
    step_count, block, _ = home_ref.shape
    cache_count = home_cache.shape[2]
    group = 8
    queries = step_count * group
    row = lax.broadcasted_iota(jnp.int32, (2 * queries, group * cache_count), 0)
    column = lax.broadcasted_iota(jnp.int32, (2 * queries, group * cache_count), 1)
    same = row % group == column // cache_count
    place = column % cache_count
    row = lax.broadcasted_iota(jnp.int32, (2 * queries, queries), 0)
    column = lax.broadcasted_iota(jnp.int32, (2 * queries, queries), 1)
    live_fresh = (row % group == column % group) & (
        column // group <= (row // group) % step_count
    )
    contract = (((1,), (1,)), ((), ()))

    def weigh(left, right, live):
        scores = lax.dot_general(left, right, contract, preferred_element_type=jnp.float32)
        scores = soft_limit * jnp.tanh(scores * (query_factor / soft_limit))
        return jnp.where(live, jnp.exp(scores), 0.0)

    for number, (items_ref, cache_ref) in enumerate(
        ((home_ref, home_cache), (back_ref, back_cache))
    ):
        items = items_ref[...].astype(jnp.float32)
        mixed = []
        for start in range(0, block, group):
            part = items[:, start : start + group].reshape(queries, -1)
            query_rows = jnp.concatenate(
                [part[:, :HEAD_SIZE], part[:, HEAD_SIZE : 2 * HEAD_SIZE]], axis=0
            ).astype(jnp.bfloat16)
            new_keys = part[:, 2 * HEAD_SIZE : 3 * HEAD_SIZE].astype(jnp.bfloat16)
            new_values = part[:, 3 * HEAD_SIZE :].astype(jnp.bfloat16)
            keys = cache_ref[0, start : start + group].reshape(group * cache_count, HEAD_SIZE)
            values = cache_ref[1, start : start + group].reshape(group * cache_count, HEAD_SIZE)
            limits = limit_ref[:, start * cache_count : (start + group) * cache_count]
            cached = weigh(query_rows, keys, same & (place < limits))
            fresh = weigh(query_rows, new_keys, live_fresh)
            share = 1.0 / (
                jnp.sum(cached, axis=1, keepdims=True) + jnp.sum(fresh, axis=1, keepdims=True)
            )
            total = jnp.dot(
                (cached * share).astype(jnp.bfloat16), values, preferred_element_type=jnp.float32
            )
            total += jnp.dot(
                (fresh * share).astype(jnp.bfloat16),
                new_values,
                preferred_element_type=jnp.float32,
            )
            mixed.append(total.reshape(2, step_count, group, HEAD_SIZE))
        for head in range(2):
            at = (2 * number + head) * HEAD_SIZE
            out_ref[:, :, at : at + HEAD_SIZE] = jnp.concatenate(
                [values[head] for values in mixed], axis=1
            ).astype(out_ref.dtype)


def attend_heads(home, back, cache, limits, heads):
    step_count, row_count, columns = home.shape
    cache_count = cache.shape[2]
    block = 16
    items = pl.BlockSpec((step_count, block, columns), lambda n, heads: (0, n, 0))

    def cached(number):
        return pl.BlockSpec(
            (2, block, cache_count, HEAD_SIZE), lambda n, heads: (0, n, 0, heads[number])
        )

    return pl.pallas_call(
        attend_kernel,
        out_shape=jax.ShapeDtypeStruct((step_count, row_count, 4 * HEAD_SIZE), jnp.bfloat16),
        grid_spec=pltpu.PrefetchScalarGridSpec(
            num_scalar_prefetch=1,
            grid=(row_count // block,),
            in_specs=[
                items,
                items,
                cached(0),
                cached(1),
                pl.BlockSpec((1, block * cache_count), lambda n, heads: (0, n)),
            ],
            out_specs=items,
        ),
        compiler_params=pltpu.CompilerParams(vmem_limit_bytes=32 * 2**20),
        cost_estimate=pl.CostEstimate(
            flops=64 * row_count * step_count * cache_count * HEAD_SIZE * 8,
            bytes_accessed=8 * row_count * cache_count * HEAD_SIZE,
            transcendentals=64 * row_count * step_count * cache_count,
        ),
    )(heads, home, back, cache, cache, limits)


def out_kernel(places, count, depth, first_ref, second_ref, *refs):
    slots = refs[: len(places)]
    kept_ref, sent_ref, mixed, weights, mixed_sems, sems = refs[len(places) :]
    half = count // 2
    front = lax.axis_index("fsdp")
    side = lax.axis_index("tp")
    core = lax.rem(lax.axis_index("grp"), 2)
    wide = 2 * HEAD_SIZE
    width = first_ref.shape[1]
    features = kept_ref.shape[1]
    copies = [
        pltpu.make_async_copy(
            mixed_ref, mixed.at[:, pl.ds(part * width, width)], mixed_sems.at[part]
        )
        for part, mixed_ref in enumerate((first_ref, second_ref))
    ]
    for number, ((k, dc), slot) in enumerate(zip(places, slots)):
        source = lax.rem(front - k + count, count)
        part = lax.rem(source // half + side, 2)
        start = pl.multiple_of(lax.rem(core + dc, 2) * depth, depth)
        for piece in range(4):
            columns = lax.rem(core + piece % 2, 2) * 2 + piece // 2
            columns = pl.multiple_of(columns * wide, wide)
            copies.append(
                pltpu.make_async_copy(
                    slot.at[:, pl.ds(columns, wide)],
                    weights.at[part, pl.ds(start, depth), pl.ds(piece * wide, wide)],
                    sems.at[number, piece],
                )
            )
    for copy in copies:
        copy.start()
    for copy in copies:
        copy.wait()
    contract = (((1,), (1,)), ((), ()))
    total = lax.dot_general(
        mixed[...], weights[1], contract, preferred_element_type=jnp.float32
    ).astype(sent_ref.dtype)
    spare = jnp.zeros((total.shape[0], sent_ref.shape[1] - features), sent_ref.dtype)
    sent_ref[...] = jnp.concatenate([total, spare], axis=1)
    kept_ref[...] = lax.dot_general(
        mixed[...], weights[0], contract, preferred_element_type=jnp.float32
    )


def out_matmul(mixed, slots, count):
    tokens, width = mixed[0].shape
    depth = slots[0][1].shape[0]
    features = 2 * depth
    padded = -(-features // 128) * 128
    return pl.pallas_call(
        functools.partial(out_kernel, [place for place, _ in slots], count, depth),
        out_shape=(
            jax.ShapeDtypeStruct((tokens, features), jnp.float32),
            jax.ShapeDtypeStruct((tokens, padded), jnp.bfloat16),
        ),
        in_specs=[pl.BlockSpec(memory_space=pltpu.HBM)] * (2 + len(slots)),
        out_specs=(pl.BlockSpec(memory_space=pltpu.VMEM),) * 2,
        scratch_shapes=[
            pltpu.VMEM((tokens, 2 * width), jnp.bfloat16),
            pltpu.VMEM((2, features, 2 * width), jnp.bfloat16),
            pltpu.SemaphoreType.DMA((2,)),
            pltpu.SemaphoreType.DMA((len(slots), 4)),
        ],
        compiler_params=pltpu.CompilerParams(vmem_limit_bytes=56 * 2**20),
        cost_estimate=pl.CostEstimate(
            flops=8 * tokens * width * features,
            bytes_accessed=8 * width * (tokens + features) + 6 * tokens * features,
            transcendentals=0,
        ),
    )(*mixed, *[values for _, values in slots])


def per_device_plane(
    count,
    hidden_states,
    pre_gain,
    post_gain,
    query_weight,
    query_mean,
    query_square,
    query_gradient,
    key_value_master_weight,
    key_value_first_moment,
    key_value_second_moment,
    key_value_gradient,
    output_weight,
    output_mean,
    output_square,
    output_gradient,
    stored_key_value_rows,
    lengths,
):
    side = lax.axis_index("tp")
    core = lax.axis_index("grp") % 2
    half = count // 2
    step_count, row_count, width = hidden_states.shape
    token_count = step_count * row_count
    group_count = stored_key_value_rows.shape[-1] // HEAD_SIZE
    cache_count = stored_key_value_rows.shape[2]
    states = hidden_states.reshape(token_count, width)

    far_states = across(states)

    def refreshed(master, mean, square, gradient):
        return adam_update(master, mean, square, gradient)[0].astype(jnp.bfloat16)

    query_arguments = (query_weight, query_mean, query_square, query_gradient)
    pair_arguments = (
        key_value_master_weight,
        key_value_first_moment,
        key_value_second_moment,
        key_value_gradient,
    )
    output_arguments = (output_weight, output_mean, output_square, output_gradient)
    query_matrix = refreshed(*query_arguments)
    pair_matrix = refreshed(*pair_arguments)
    output_matrix = refreshed(*output_arguments)

    near_half = group_count // 2

    def head_part(group):
        return jnp.concatenate(
            [
                query_matrix[:, group * 2 * HEAD_SIZE : (group + 1) * 2 * HEAD_SIZE],
                pair_matrix[:, 0, group * HEAD_SIZE : (group + 1) * HEAD_SIZE],
                pair_matrix[:, 1, group * HEAD_SIZE : (group + 1) * HEAD_SIZE],
            ],
            axis=1,
        )

    low = jnp.concatenate([head_part(0), head_part(1)], axis=1)
    high = jnp.concatenate([head_part(near_half), head_part(near_half + 1)], axis=1)
    kept = jnp.where(core == 0, low, high)
    taken = flip(jnp.where(core == 0, high, low), 1)
    middle = 4 * HEAD_SIZE
    blocks = [
        jnp.concatenate([kept[:, :middle], taken[:, :middle]], axis=0),
        jnp.concatenate([kept[:, middle:], taken[:, middle:]], axis=0),
    ]

    lanes = Lanes(count)
    first = {(0, 0): blocks[0]}
    second = {(0, 0): blocks[1]}
    for k in range(count):
        for part in (first, second):
            if k:
                part[k, 0] = lanes.ring(part[k - 1, 0])
        for part in (first, second):
            part[k, 1] = lanes.swap(part[k, 0])

    near = states.astype(jnp.float32)
    far = after(far_states, second[1, 1]).astype(jnp.float32)
    mean_square = (
        jnp.sum(near * near, axis=1, keepdims=True) + jnp.sum(far * far, axis=1, keepdims=True)
    ) / (2 * width)
    scale = lax.rsqrt(mean_square + norm_epsilon)
    near_gain = lax.dynamic_slice_in_dim(pre_gain, side * width, width)
    far_gain = lax.dynamic_slice_in_dim(pre_gain, (1 - side) * width, width)
    near_normed = (near * scale * near_gain).astype(jnp.bfloat16)
    far_normed = (far * scale * far_gain).astype(jnp.bfloat16)
    near_away = flip(near_normed, 1)
    far_away = flip(far_normed, 1)

    query_next = adam_update(after(query_weight, second[2, 1]), *query_arguments[1:])
    key_value_following = adam_update(after(pair_arguments[0], second[2, 1]), *pair_arguments[1:])
    output_next = adam_update(after(output_weight, second[2, 1]), *output_arguments[1:])

    limits = jnp.repeat(lengths, cache_count)[None, :]

    def project(slots):
        slots = [(*place, slots[place]) for place in slots]
        away, home = qkv_matmul((near_away, far_away), (near_normed, far_normed), slots, count)
        return home, flip(away, 1)

    def attention(home, back, part):
        return attend_heads(
            home.reshape(step_count, row_count, -1),
            back.reshape(step_count, row_count, -1),
            stored_key_value_rows,
            limits,
            jnp.stack([core * near_half + part, (1 - core) * near_half + part]),
        ).reshape(token_count, -1)

    third = {(0, 0, 0): output_matrix}

    def cores(k, dy, *others):
        third[k, dy, 1] = flip(after(third[k, dy, 0], *others) if others else third[k, dy, 0], 1)
        return third[k, dy, 1]

    def project_out(parity, dy):
        slots = [
            ((k, dc), third[k, dy, dc]) for k in range(parity, count, 2) for dc in range(2)
        ]
        return out_matmul([first_mixed, second_mixed], slots, count)

    third[1, 0, 0] = lanes.ring(output_matrix)
    third[2, 0, 0] = lanes.ring(third[1, 0, 0], near_away, far_away)
    third[0, 1, 0] = lanes.swap(output_matrix)
    first_heads = project(first)
    third[3, 0, 0] = lanes.ring(third[2, 0, 0], first_heads[0])
    third[1, 1, 0] = lanes.swap(third[1, 0, 0], cores(0, 0), *first_heads)
    second_heads = project(second)
    first_mixed = attention(*first_heads, 0)
    third[2, 1, 0] = lanes.swap(third[2, 0, 0], cores(1, 0), first_mixed, *second_heads)
    second_mixed = attention(*second_heads, 1)
    third[3, 1, 0] = lanes.swap(third[3, 0, 0], cores(0, 1), cores(2, 0), second_mixed)
    cores(3, 0)
    sent = {}
    parts = {}
    for parity in range(2):
        parts[parity, 0] = project_out(parity, 0)
        sent[parity, 0] = across(parts[parity, 0][1])
    cores(1, 1)
    cores(2, 1, sent[0, 0], *parts[1, 0])
    parts[0, 1] = project_out(0, 1)
    sent[0, 1] = across(parts[0, 1][1])
    cores(3, 1, *query_next, *key_value_following, *output_next, sent[1, 0], *parts[0, 1])
    parts[1, 1] = project_out(1, 1)
    sent[1, 1] = across(parts[1, 1][1])
    sums = {
        place: kept + sent[place][:, : kept.shape[1]].astype(jnp.float32)
        for place, (kept, _) in parts.items()
    }
    squares = sum(
        jnp.sum(values * values, axis=1, keepdims=True) for values in sums.values()
    )
    square_total = squares + across(squares)
    inverse = lax.rsqrt(square_total / (2 * width) + norm_epsilon)
    top = lax.axis_index("grp") // 2 == 0
    even = lax.axis_index("fsdp") % 2 == 0
    halves = [
        jnp.concatenate(
            [
                jnp.where(top, sums[parity, 0], sums[parity, 1]),
                jnp.where(top, sums[parity, 1], sums[parity, 0]),
            ],
            axis=1,
        )
        for parity in range(2)
    ]
    projected = jnp.concatenate(
        [jnp.where(even, halves[0], halves[1]), jnp.where(even, halves[1], halves[0])], axis=1
    )
    branch = projected * inverse * post_gain
    rollout_states = (states.astype(jnp.float32) + branch).astype(jnp.bfloat16)
    return (
        rollout_states.reshape(hidden_states.shape),
        *query_next,
        *key_value_following,
        *output_next,
    )


def plan_for(mesh, depth, groups):
    sizes = dict(mesh.shape)
    count = sizes["fsdp"]
    rows = depth // (count * sizes["grp"])
    if sizes == {"fsdp": 4, "tp": 2, "grp": 4} and groups == 4 and rows % 96 == 0:
        return functools.partial(per_device_plane, count)
    return per_device


def solution(mesh):
    placed = (
        P(None, ("fsdp", "grp"), "tp"),
        P(),
        P("tp"),
        P(("fsdp", "grp"), "tp"),
        P(("fsdp", "grp"), "tp"),
        P(("fsdp", "grp"), "tp"),
        P(("fsdp", "grp"), "tp"),
        P(("fsdp", "grp"), None, "tp"),
        P(("fsdp", "grp"), None, "tp"),
        P(("fsdp", "grp"), None, "tp"),
        P(("fsdp", "grp"), None, "tp"),
        P(("fsdp", "grp"), "tp"),
        P(("fsdp", "grp"), "tp"),
        P(("fsdp", "grp"), "tp"),
        P(("fsdp", "grp"), "tp"),
        P(None, ("fsdp", "grp"), None, "tp"),
        P(("fsdp", "grp")),
    )
    mapped = functools.partial(
        jax.shard_map,
        mesh=mesh,
        in_specs=placed,
        out_specs=(
            P(None, ("fsdp", "grp"), "tp"),
            P(("fsdp", "grp"), "tp"),
            P(("fsdp", "grp"), "tp"),
            P(("fsdp", "grp"), "tp"),
            P(("fsdp", "grp"), None, "tp"),
            P(("fsdp", "grp"), None, "tp"),
            P(("fsdp", "grp"), None, "tp"),
            P(("fsdp", "grp"), "tp"),
            P(("fsdp", "grp"), "tp"),
            P(("fsdp", "grp"), "tp"),
        ),
        check_vma=False,
    )

    def step(*args):
        return mapped(plan_for(mesh, args[3].shape[0], args[15].shape[3] // HEAD_SIZE // mesh.shape["tp"]))(*args)

    return step
```

```python
import functools

import jax
import jax.numpy as jnp
from jax import lax
from jax.experimental import pallas as pl
from jax.experimental.pallas import tpu as pltpu
from jax.sharding import PartitionSpec as P

HEAD_SIZE = 128


beta_first = 0.9
beta_second = 0.95
learning_rate = 0.001
update_number = 100
soft_limit = 50.0
query_factor = 144.0 ** (-0.5)
norm_epsilon = 1e-06


def adam_update(master, moment_mean, moment_square, gradient):
    gradient_float = gradient.astype(jnp.float32)
    mean_next = beta_first * moment_mean + (1.0 - beta_first) * gradient_float
    square_next = (
        beta_second * moment_square + (1.0 - beta_second) * gradient_float * gradient_float
    )
    mean_hat = mean_next / (1.0 - beta_first**update_number)
    square_hat = square_next / (1.0 - beta_second**update_number)
    master_next = master - learning_rate * mean_hat / jnp.sqrt(square_hat)
    return (master_next, mean_next, square_next)


def rms_apply(values, gains):
    mean_square = jnp.mean(values * values, axis=-1, keepdims=True) + norm_epsilon
    return values * lax.rsqrt(mean_square) * gains


def attend(query_rows, new_keys, new_values, cache_keys, cache_values, lengths):
    step_count = query_rows.shape[0]
    cache_count = cache_keys.shape[1]
    score_cache = jnp.einsum(
        "trgqd,rcgd->trgqc", query_rows, cache_keys, preferred_element_type=jnp.float32
    )
    score_fresh = jnp.einsum(
        "trgqd,srgd->trgqs", query_rows, new_keys, preferred_element_type=jnp.float32
    )
    score_cache = soft_limit * jnp.tanh(score_cache * query_factor / soft_limit)
    score_fresh = soft_limit * jnp.tanh(score_fresh * query_factor / soft_limit)
    live_cache = jnp.arange(cache_count, dtype=jnp.int32)[None, :] < lengths[:, None]
    positions = jnp.arange(step_count, dtype=jnp.int32)
    live_fresh = positions[None, :] <= positions[:, None]
    weight_cache = jnp.where(live_cache[None, :, None, None, :], jnp.exp(score_cache), 0.0)
    weight_fresh = jnp.where(live_fresh[:, None, None, None, :], jnp.exp(score_fresh), 0.0)
    totals = jnp.sum(weight_cache, axis=-1, keepdims=True) + jnp.sum(
        weight_fresh, axis=-1, keepdims=True
    )
    prob_cache = (weight_cache / totals).astype(jnp.bfloat16)
    prob_fresh = (weight_fresh / totals).astype(jnp.bfloat16)
    mixed = jnp.einsum(
        "trgqc,rcgd->trgqd", prob_cache, cache_values, preferred_element_type=jnp.float32
    )
    mixed = mixed + jnp.einsum(
        "trgqs,srgd->trgqd", prob_fresh, new_values, preferred_element_type=jnp.float32
    )
    return mixed.astype(jnp.bfloat16)


def per_device(
    hidden_states,
    pre_gain,
    post_gain,
    query_weight,
    query_mean,
    query_square,
    query_gradient,
    key_value_master_weight,
    key_value_first_moment,
    key_value_second_moment,
    key_value_gradient,
    output_weight,
    output_mean,
    output_square,
    output_gradient,
    stored_key_value_rows,
    lengths,
):
    query_next = adam_update(query_weight, query_mean, query_square, query_gradient)
    key_value_following = adam_update(
        key_value_master_weight, key_value_first_moment, key_value_second_moment, key_value_gradient
    )
    output_next = adam_update(output_weight, output_mean, output_square, output_gradient)
    query_matrix = query_next[0].astype(jnp.bfloat16)
    key_value_matrix = key_value_following[0].astype(jnp.bfloat16)
    key_value_matrix = key_value_matrix.reshape(key_value_matrix.shape[0], -1)
    output_matrix = output_next[0].astype(jnp.bfloat16)
    gathered = lax.all_gather(hidden_states, "tp", axis=2, tiled=True)
    step_count, row_count, full_width = gathered.shape
    token_count = step_count * row_count
    normed = (
        rms_apply(gathered.astype(jnp.float32), pre_gain)
        .astype(jnp.bfloat16)
        .reshape(token_count, full_width)
    )
    query_sum = jnp.dot(
        normed,
        lax.all_gather(query_matrix, ("fsdp", "grp"), axis=0, tiled=True),
        preferred_element_type=jnp.float32,
    )
    pair_sum = jnp.dot(
        normed,
        lax.all_gather(key_value_matrix, ("fsdp", "grp"), axis=0, tiled=True),
        preferred_element_type=jnp.float32,
    )
    group_count = stored_key_value_rows.shape[-1] // HEAD_SIZE
    cache_count = stored_key_value_rows.shape[2]
    query_rows = query_sum.astype(jnp.bfloat16).reshape(
        step_count, row_count, group_count, 2, HEAD_SIZE
    )
    key_value_items = pair_sum.astype(jnp.bfloat16).reshape(
        step_count, row_count, 2, group_count, HEAD_SIZE
    )
    cache_division = stored_key_value_rows.reshape(
        2, row_count, cache_count, group_count, HEAD_SIZE
    )
    mixed = attend(
        query_rows,
        key_value_items[:, :, 0],
        key_value_items[:, :, 1],
        cache_division[0],
        cache_division[1],
        lengths,
    )
    mixed = mixed.reshape(token_count, group_count * 2 * HEAD_SIZE)
    projected = lax.dot_general(
        mixed,
        lax.all_gather(output_matrix, ("fsdp", "grp"), axis=0, tiled=True),
        (((1,), (1,)), ((), ())),
        preferred_element_type=jnp.float32,
    )
    shares = lax.psum_scatter(projected, "tp", scatter_dimension=1, tiled=True)
    row_squares = jnp.sum(shares * shares, axis=1)
    square_total = lax.psum(row_squares, "tp")
    inverse = lax.rsqrt(square_total / full_width + norm_epsilon)
    branch = shares * inverse[:, None] * post_gain
    rollout_states = (
        hidden_states.astype(jnp.float32) + branch.reshape(step_count, row_count, -1)
    ).astype(jnp.bfloat16)
    return (
        rollout_states,
        query_next[0],
        query_next[1],
        query_next[2],
        key_value_following[0],
        key_value_following[1],
        key_value_following[2],
        output_next[0],
        output_next[1],
        output_next[2],
    )


def flip(values, bit):
    return lax.ppermute(values, "grp", [(i, i ^ bit) for i in range(4)])


def across(values):
    return lax.ppermute(values, "tp", [(0, 1), (1, 0)])


def after(values, *others):
    return lax.optimization_barrier((values, *others))[0]


class Lanes:
    def __init__(self, count):
        self.count = count
        self.along_z = []
        self.along_y = []

    def ring(self, values, *others):
        step = len(self.along_z)
        waits = self.along_y[step - 2 : step - 1] if step > 1 else []
        values = after(values, *self.along_z[-2:-1], *waits, *others)
        moves = [(i, (i + 1) % self.count) for i in range(self.count)]
        self.along_z.append(lax.ppermute(values, "fsdp", moves))
        return self.along_z[-1]

    def swap(self, values, *others):
        values = after(values, *self.along_y[-2:-1], *others)
        self.along_y.append(flip(values, 2))
        return self.along_y[-1]


def qkv_kernel(places, count, depth, *refs):
    inputs, slots = refs[:4], refs[4 : 4 + len(places)]
    away_ref, home_ref, tokens, weights, token_sems, sems = refs[4 + len(places) :]
    half = count // 2
    front = lax.axis_index("fsdp")
    side = lax.axis_index("tp")
    inner = lax.axis_index("grp")
    row, core = inner // 2, lax.rem(inner, 2)
    tiles, _, tile = weights.shape
    width = inputs[0].shape[1]

    def bring_tokens(group):
        for part in range(2):
            yield pltpu.make_async_copy(
                inputs[2 * group + part],
                tokens.at[group, :, pl.ds(part * width, width)],
                token_sems.at[group, part],
            )

    def bring_weights(index):
        for number, ((k, dy), slot) in enumerate(zip(places, slots)):
            source = lax.rem(front - k + count, count)
            part = lax.rem(source // half + side, 2)
            base = (part * half + lax.rem(source, half)) * 4 + lax.rem(row + dy, 2) * 2
            for dc in range(2):
                start = pl.multiple_of((base + lax.rem(core + dc, 2)) * depth, depth)
                yield pltpu.make_async_copy(
                    slot.at[pl.ds(dc * depth, depth), pl.ds(index * tile, tile)],
                    weights.at[index, pl.ds(start, depth), :],
                    sems.at[index, number * 2 + dc],
                )

    def start(copies):
        for copy in copies:
            copy.start()

    def wait(copies):
        for copy in copies:
            copy.wait()

    start(bring_weights(0))
    start(bring_tokens(0))
    for group, out_ref in enumerate((away_ref, home_ref)):
        wait(bring_tokens(group))
        for index in range(tiles):
            if group == 0:
                wait(bring_weights(index))
                if index + 1 < tiles:
                    start(bring_weights(index + 1))
                else:
                    start(bring_tokens(1))
            out_ref[:, index * tile : (index + 1) * tile] = jnp.dot(
                tokens[group], weights[index], preferred_element_type=jnp.float32
            ).astype(out_ref.dtype)


def qkv_matmul(away, home, slots, count):
    tokens, width = home[0].shape
    depth, columns = slots[0][2].shape[0] // 2, slots[0][2].shape[1]
    tile = 256
    return pl.pallas_call(
        functools.partial(qkv_kernel, [(k, dy) for k, dy, _ in slots], count, depth),
        out_shape=(jax.ShapeDtypeStruct((tokens, columns), jnp.bfloat16),) * 2,
        in_specs=[pl.BlockSpec(memory_space=pltpu.HBM)] * (4 + len(slots)),
        out_specs=(pl.BlockSpec(memory_space=pltpu.VMEM),) * 2,
        scratch_shapes=[
            pltpu.VMEM((2, tokens, 2 * width), jnp.bfloat16),
            pltpu.VMEM((columns // tile, 2 * width, tile), jnp.bfloat16),
            pltpu.SemaphoreType.DMA((2, 2)),
            pltpu.SemaphoreType.DMA((columns // tile, 2 * len(slots))),
        ],
        compiler_params=pltpu.CompilerParams(vmem_limit_bytes=56 * 2**20),
        cost_estimate=pl.CostEstimate(
            flops=8 * tokens * width * columns,
            bytes_accessed=4 * width * (2 * tokens + columns) + 4 * tokens * columns,
            transcendentals=0,
        ),
    )(*away, *home, *[values for _, _, values in slots])


def attend_kernel(heads_ref, home_ref, back_ref, home_cache, back_cache, limit_ref, out_ref):
    step_count, block, _ = home_ref.shape
    cache_count = home_cache.shape[2]
    group = 8
    queries = step_count * group
    row = lax.broadcasted_iota(jnp.int32, (2 * queries, group * cache_count), 0)
    column = lax.broadcasted_iota(jnp.int32, (2 * queries, group * cache_count), 1)
    same = row % group == column // cache_count
    place = column % cache_count
    row = lax.broadcasted_iota(jnp.int32, (2 * queries, queries), 0)
    column = lax.broadcasted_iota(jnp.int32, (2 * queries, queries), 1)
    live_fresh = (row % group == column % group) & (
        column // group <= (row // group) % step_count
    )
    contract = (((1,), (1,)), ((), ()))

    def weigh(left, right, live):
        scores = lax.dot_general(left, right, contract, preferred_element_type=jnp.float32)
        scores = soft_limit * jnp.tanh(scores * (query_factor / soft_limit))
        return jnp.where(live, jnp.exp(scores), 0.0)

    for number, (items_ref, cache_ref) in enumerate(
        ((home_ref, home_cache), (back_ref, back_cache))
    ):
        items = items_ref[...].astype(jnp.float32)
        mixed = []
        for start in range(0, block, group):
            part = items[:, start : start + group].reshape(queries, -1)
            query_rows = jnp.concatenate(
                [part[:, :HEAD_SIZE], part[:, HEAD_SIZE : 2 * HEAD_SIZE]], axis=0
            ).astype(jnp.bfloat16)
            new_keys = part[:, 2 * HEAD_SIZE : 3 * HEAD_SIZE].astype(jnp.bfloat16)
            new_values = part[:, 3 * HEAD_SIZE :].astype(jnp.bfloat16)
            keys = cache_ref[0, start : start + group].reshape(group * cache_count, HEAD_SIZE)
            values = cache_ref[1, start : start + group].reshape(group * cache_count, HEAD_SIZE)
            limits = limit_ref[:, start * cache_count : (start + group) * cache_count]
            cached = weigh(query_rows, keys, same & (place < limits))
            fresh = weigh(query_rows, new_keys, live_fresh)
            share = 1.0 / (
                jnp.sum(cached, axis=1, keepdims=True) + jnp.sum(fresh, axis=1, keepdims=True)
            )
            total = jnp.dot(
                (cached * share).astype(jnp.bfloat16), values, preferred_element_type=jnp.float32
            )
            total += jnp.dot(
                (fresh * share).astype(jnp.bfloat16),
                new_values,
                preferred_element_type=jnp.float32,
            )
            mixed.append(total.reshape(2, step_count, group, HEAD_SIZE))
        for head in range(2):
            at = (2 * number + head) * HEAD_SIZE
            out_ref[:, :, at : at + HEAD_SIZE] = jnp.concatenate(
                [values[head] for values in mixed], axis=1
            ).astype(out_ref.dtype)


def attend_heads(home, back, cache, limits, heads):
    step_count, row_count, columns = home.shape
    cache_count = cache.shape[2]
    block = 16
    items = pl.BlockSpec((step_count, block, columns), lambda n, heads: (0, n, 0))

    def cached(number):
        return pl.BlockSpec(
            (2, block, cache_count, HEAD_SIZE), lambda n, heads: (0, n, 0, heads[number])
        )

    return pl.pallas_call(
        attend_kernel,
        out_shape=jax.ShapeDtypeStruct((step_count, row_count, 4 * HEAD_SIZE), jnp.bfloat16),
        grid_spec=pltpu.PrefetchScalarGridSpec(
            num_scalar_prefetch=1,
            grid=(row_count // block,),
            in_specs=[
                items,
                items,
                cached(0),
                cached(1),
                pl.BlockSpec((1, block * cache_count), lambda n, heads: (0, n)),
            ],
            out_specs=items,
        ),
        compiler_params=pltpu.CompilerParams(vmem_limit_bytes=32 * 2**20),
        cost_estimate=pl.CostEstimate(
            flops=64 * row_count * step_count * cache_count * HEAD_SIZE * 8,
            bytes_accessed=8 * row_count * cache_count * HEAD_SIZE,
            transcendentals=64 * row_count * step_count * cache_count,
        ),
    )(heads, home, back, cache, cache, limits)


def out_kernel(places, count, depth, first_ref, second_ref, *refs):
    slots = refs[: len(places)]
    kept_ref, sent_ref, mixed, weights, mixed_sems, sems = refs[len(places) :]
    half = count // 2
    front = lax.axis_index("fsdp")
    side = lax.axis_index("tp")
    core = lax.rem(lax.axis_index("grp"), 2)
    wide = 2 * HEAD_SIZE
    width = first_ref.shape[1]
    features = kept_ref.shape[1]
    copies = [
        pltpu.make_async_copy(
            mixed_ref, mixed.at[:, pl.ds(part * width, width)], mixed_sems.at[part]
        )
        for part, mixed_ref in enumerate((first_ref, second_ref))
    ]
    for number, ((k, dc), slot) in enumerate(zip(places, slots)):
        source = lax.rem(front - k + count, count)
        part = lax.rem(source // half + side, 2)
        start = pl.multiple_of(lax.rem(core + dc, 2) * depth, depth)
        for piece in range(4):
            columns = lax.rem(core + piece % 2, 2) * 2 + piece // 2
            columns = pl.multiple_of(columns * wide, wide)
            copies.append(
                pltpu.make_async_copy(
                    slot.at[:, pl.ds(columns, wide)],
                    weights.at[part, pl.ds(start, depth), pl.ds(piece * wide, wide)],
                    sems.at[number, piece],
                )
            )
    for copy in copies:
        copy.start()
    for copy in copies:
        copy.wait()
    contract = (((1,), (1,)), ((), ()))
    total = lax.dot_general(
        mixed[...], weights[1], contract, preferred_element_type=jnp.float32
    ).astype(sent_ref.dtype)
    spare = jnp.zeros((total.shape[0], sent_ref.shape[1] - features), sent_ref.dtype)
    sent_ref[...] = jnp.concatenate([total, spare], axis=1)
    kept_ref[...] = lax.dot_general(
        mixed[...], weights[0], contract, preferred_element_type=jnp.float32
    )


def out_matmul(mixed, slots, count):
    tokens, width = mixed[0].shape
    depth = slots[0][1].shape[0]
    features = 2 * depth
    padded = -(-features // 128) * 128
    return pl.pallas_call(
        functools.partial(out_kernel, [place for place, _ in slots], count, depth),
        out_shape=(
            jax.ShapeDtypeStruct((tokens, features), jnp.float32),
            jax.ShapeDtypeStruct((tokens, padded), jnp.bfloat16),
        ),
        in_specs=[pl.BlockSpec(memory_space=pltpu.HBM)] * (2 + len(slots)),
        out_specs=(pl.BlockSpec(memory_space=pltpu.VMEM),) * 2,
        scratch_shapes=[
            pltpu.VMEM((tokens, 2 * width), jnp.bfloat16),
            pltpu.VMEM((2, features, 2 * width), jnp.bfloat16),
            pltpu.SemaphoreType.DMA((2,)),
            pltpu.SemaphoreType.DMA((len(slots), 4)),
        ],
        compiler_params=pltpu.CompilerParams(vmem_limit_bytes=56 * 2**20),
        cost_estimate=pl.CostEstimate(
            flops=8 * tokens * width * features,
            bytes_accessed=8 * width * (tokens + features) + 6 * tokens * features,
            transcendentals=0,
        ),
    )(*mixed, *[values for _, values in slots])


def per_device_plane(
    count,
    hidden_states,
    pre_gain,
    post_gain,
    query_weight,
    query_mean,
    query_square,
    query_gradient,
    key_value_master_weight,
    key_value_first_moment,
    key_value_second_moment,
    key_value_gradient,
    output_weight,
    output_mean,
    output_square,
    output_gradient,
    stored_key_value_rows,
    lengths,
):
    side = lax.axis_index("tp")
    core = lax.axis_index("grp") % 2
    half = count // 2
    step_count, row_count, width = hidden_states.shape
    token_count = step_count * row_count
    group_count = stored_key_value_rows.shape[-1] // HEAD_SIZE
    cache_count = stored_key_value_rows.shape[2]
    states = hidden_states.reshape(token_count, width)

    far_states = across(states)

    def refreshed(master, mean, square, gradient):
        return adam_update(master, mean, square, gradient)[0].astype(jnp.bfloat16)

    query_arguments = (query_weight, query_mean, query_square, query_gradient)
    pair_arguments = (
        key_value_master_weight,
        key_value_first_moment,
        key_value_second_moment,
        key_value_gradient,
    )
    output_arguments = (output_weight, output_mean, output_square, output_gradient)
    query_matrix = refreshed(*query_arguments)
    pair_matrix = refreshed(*pair_arguments)
    output_matrix = refreshed(*output_arguments)

    near_half = group_count // 2

    def head_part(group):
        return jnp.concatenate(
            [
                query_matrix[:, group * 2 * HEAD_SIZE : (group + 1) * 2 * HEAD_SIZE],
                pair_matrix[:, 0, group * HEAD_SIZE : (group + 1) * HEAD_SIZE],
                pair_matrix[:, 1, group * HEAD_SIZE : (group + 1) * HEAD_SIZE],
            ],
            axis=1,
        )

    low = jnp.concatenate([head_part(0), head_part(1)], axis=1)
    high = jnp.concatenate([head_part(near_half), head_part(near_half + 1)], axis=1)
    kept = jnp.where(core == 0, low, high)
    taken = flip(jnp.where(core == 0, high, low), 1)
    middle = 4 * HEAD_SIZE
    blocks = [
        jnp.concatenate([kept[:, :middle], taken[:, :middle]], axis=0),
        jnp.concatenate([kept[:, middle:], taken[:, middle:]], axis=0),
    ]

    lanes = Lanes(count)
    first = {(0, 0): blocks[0]}
    second = {(0, 0): blocks[1]}
    for k in range(count):
        for part in (first, second):
            if k:
                part[k, 0] = lanes.ring(part[k - 1, 0])
        for part in (first, second):
            part[k, 1] = lanes.swap(part[k, 0])

    near = states.astype(jnp.float32)
    far = after(far_states, second[1, 1]).astype(jnp.float32)
    mean_square = (
        jnp.sum(near * near, axis=1, keepdims=True) + jnp.sum(far * far, axis=1, keepdims=True)
    ) / (2 * width)
    scale = lax.rsqrt(mean_square + norm_epsilon)
    near_gain = lax.dynamic_slice_in_dim(pre_gain, side * width, width)
    far_gain = lax.dynamic_slice_in_dim(pre_gain, (1 - side) * width, width)
    near_normed = (near * scale * near_gain).astype(jnp.bfloat16)
    far_normed = (far * scale * far_gain).astype(jnp.bfloat16)
    near_away = flip(near_normed, 1)
    far_away = flip(far_normed, 1)

    query_next = adam_update(after(query_weight, second[2, 1]), *query_arguments[1:])
    key_value_following = adam_update(after(pair_arguments[0], second[2, 1]), *pair_arguments[1:])
    output_next = adam_update(after(output_weight, second[2, 1]), *output_arguments[1:])

    limits = jnp.repeat(lengths, cache_count)[None, :]

    def project(slots):
        slots = [(*place, slots[place]) for place in slots]
        away, home = qkv_matmul((near_away, far_away), (near_normed, far_normed), slots, count)
        return home, flip(away, 1)

    def attention(home, back, part):
        return attend_heads(
            home.reshape(step_count, row_count, -1),
            back.reshape(step_count, row_count, -1),
            stored_key_value_rows,
            limits,
            jnp.stack([core * near_half + part, (1 - core) * near_half + part]),
        ).reshape(token_count, -1)

    third = {(0, 0, 0): output_matrix}

    def cores(k, dy, *others):
        third[k, dy, 1] = flip(after(third[k, dy, 0], *others) if others else third[k, dy, 0], 1)
        return third[k, dy, 1]

    def project_out(parity, dy):
        slots = [
            ((k, dc), third[k, dy, dc]) for k in range(parity, count, 2) for dc in range(2)
        ]
        return out_matmul([first_mixed, second_mixed], slots, count)

    third[1, 0, 0] = lanes.ring(output_matrix)
    third[2, 0, 0] = lanes.ring(third[1, 0, 0], near_away, far_away)
    third[0, 1, 0] = lanes.swap(output_matrix)
    first_heads = project(first)
    third[3, 0, 0] = lanes.ring(third[2, 0, 0])
    third[1, 1, 0] = lanes.swap(third[1, 0, 0], cores(0, 0), *first_heads)
    second_heads = project(second)
    first_mixed = attention(*first_heads, 0)
    third[2, 1, 0] = lanes.swap(third[2, 0, 0], cores(1, 0), first_mixed, *second_heads)
    second_mixed = attention(*second_heads, 1)
    third[3, 1, 0] = lanes.swap(third[3, 0, 0], cores(0, 1), cores(2, 0), second_mixed)
    cores(3, 0)
    sent = {}
    parts = {}
    for parity in range(2):
        parts[parity, 0] = project_out(parity, 0)
        sent[parity, 0] = across(parts[parity, 0][1])
    cores(1, 1)
    cores(2, 1, sent[0, 0], *parts[1, 0])
    parts[0, 1] = project_out(0, 1)
    sent[0, 1] = across(parts[0, 1][1])
    cores(3, 1, *query_next, *key_value_following, *output_next, sent[1, 0], *parts[0, 1])
    parts[1, 1] = project_out(1, 1)
    sent[1, 1] = across(parts[1, 1][1])
    sums = {
        place: kept + sent[place][:, : kept.shape[1]].astype(jnp.float32)
        for place, (kept, _) in parts.items()
    }
    squares = sum(
        jnp.sum(values * values, axis=1, keepdims=True) for values in sums.values()
    )
    square_total = squares + across(squares)
    inverse = lax.rsqrt(square_total / (2 * width) + norm_epsilon)
    top = lax.axis_index("grp") // 2 == 0
    even = lax.axis_index("fsdp") % 2 == 0
    halves = [
        jnp.concatenate(
            [
                jnp.where(top, sums[parity, 0], sums[parity, 1]),
                jnp.where(top, sums[parity, 1], sums[parity, 0]),
            ],
            axis=1,
        )
        for parity in range(2)
    ]
    projected = jnp.concatenate(
        [jnp.where(even, halves[0], halves[1]), jnp.where(even, halves[1], halves[0])], axis=1
    )
    branch = projected * inverse * post_gain
    rollout_states = (states.astype(jnp.float32) + branch).astype(jnp.bfloat16)
    return (
        rollout_states.reshape(hidden_states.shape),
        *query_next,
        *key_value_following,
        *output_next,
    )


def plan_for(mesh, depth, groups):
    sizes = dict(mesh.shape)
    count = sizes["fsdp"]
    rows = depth // (count * sizes["grp"])
    if sizes == {"fsdp": 4, "tp": 2, "grp": 4} and groups == 4 and rows % 96 == 0:
        return functools.partial(per_device_plane, count)
    return per_device


def solution(mesh):
    placed = (
        P(None, ("fsdp", "grp"), "tp"),
        P(),
        P("tp"),
        P(("fsdp", "grp"), "tp"),
        P(("fsdp", "grp"), "tp"),
        P(("fsdp", "grp"), "tp"),
        P(("fsdp", "grp"), "tp"),
        P(("fsdp", "grp"), None, "tp"),
        P(("fsdp", "grp"), None, "tp"),
        P(("fsdp", "grp"), None, "tp"),
        P(("fsdp", "grp"), None, "tp"),
        P(("fsdp", "grp"), "tp"),
        P(("fsdp", "grp"), "tp"),
        P(("fsdp", "grp"), "tp"),
        P(("fsdp", "grp"), "tp"),
        P(None, ("fsdp", "grp"), None, "tp"),
        P(("fsdp", "grp")),
    )
    mapped = functools.partial(
        jax.shard_map,
        mesh=mesh,
        in_specs=placed,
        out_specs=(
            P(None, ("fsdp", "grp"), "tp"),
            P(("fsdp", "grp"), "tp"),
            P(("fsdp", "grp"), "tp"),
            P(("fsdp", "grp"), "tp"),
            P(("fsdp", "grp"), None, "tp"),
            P(("fsdp", "grp"), None, "tp"),
            P(("fsdp", "grp"), None, "tp"),
            P(("fsdp", "grp"), "tp"),
            P(("fsdp", "grp"), "tp"),
            P(("fsdp", "grp"), "tp"),
        ),
        check_vma=False,
    )

    def step(*args):
        return mapped(plan_for(mesh, args[3].shape[0], args[15].shape[3] // HEAD_SIZE // mesh.shape["tp"]))(*args)

    return step
```
